256 devices in a mesh: dp: 4 (over y), pipe: 8 (over z_lo, x), tensor: 8 (over z_hi, core).
Axes of the slice: x: 4, y: 4, z: 8 (z_hi: 4, z_lo: 2; z = z_hi * 2 + z_lo), core: 2. Of those that a mesh axis runs over, the one named last changes fastest.
Arguments:
- token_ids: int32 [2048], P(('dp', 'pipe')), may hold values from 0 to 50256
- head_input: bfloat16 [2048, 12288], P('pipe', 'dp'), may hold values from -6 to 6
- embed_grad: bfloat16 [2048, 12288], P('pipe', 'dp'), may hold values from -4 to 4
- logit_grad: bfloat16 [2048, 51200], P(('dp', 'pipe'), 'tensor'), may hold values from -0.125 to 0.125
Outputs:
- tied_grad: bfloat16 [51200, 12288], P('tensor', ('dp', 'pipe'))
The draws below stay inside these ranges and needn't reach their ends.
Inputs may be any that keep to these rules, and one draw needn't show every extreme that they name: `token_ids`: every id names a real vocabulary entry, never a padding row.
All inputs are finite; a program needn't handle non-finite values.
Results may differ from the reference program's by a relative error of at most 0.001.
Values may be sent and summed in bfloat16 or wider, within the bound.
No kernel may reach another device: no remote copies, remote signals or barrier semaphores. Data moves between devices by JAX's collectives and lax.ppermute only.
A program may use at most 128 MiB of HBM per device.

```python
import math
import jax
import jax.numpy as jnp
import numpy as np
from jax import lax

D = 12288
VOCAB = 51200
VALID = 50257
TOKENS = 2048
N_TENSOR = 8


def with_ends(array, rng, low, largest):
    longest = array.shape.index(max(array.shape))
    spots = []
    for shift in (0, 1):
        where = [jax.random.randint(jax.random.fold_in(rng, axis), (), 0, length) for axis, length in enumerate(array.shape)]
        where[longest] = (where[longest] + shift) % array.shape[longest]
        spots.append(tuple(where))
    return array.at[spots[0]].set(low).at[spots[1]].set(largest)


def level_of(key, dims, cuts, low, high):
    gain, own = 1.0, jax.random.fold_in(key, 6)
    for axis_at, parts in cuts:
        heights = jnp.exp(jax.random.uniform(jax.random.fold_in(own, axis_at), (parts,), jnp.float32, low / len(cuts), high / len(cuts)))
        gain = gain * jnp.repeat(heights, dims[axis_at] // parts).reshape([-1 if axis == axis_at else 1 for axis in range(len(dims))])
    return gain


def rank_table(number_of, slope):
    portions = [(1 << 20) // math.isqrt(standing ** slope) + 1 for standing in range(1, number_of + 1)]
    deviation = 1 + sum(portions) // (1 << 30)
    return np.cumsum(np.array([max(1, weight // deviation) for weight in portions]))


def ranked(rng, dims, number_of, slope):
    listing = rank_table(number_of, slope)
    ticket = jax.random.randint(jax.random.fold_in(rng, 1), dims, 0, int(listing[number_of - 1]))
    grade = jnp.searchsorted(jnp.asarray(listing, jnp.int32), ticket, side="right")
    return jax.random.permutation(jax.random.fold_in(rng, 2), number_of)[grade].astype(jnp.int32)


def noise(rng, shape, scale, most, pieces=(), held_as=jnp.bfloat16):
    level = level_of(rng, shape, pieces, -0.22, 0.18) if pieces else 1.0
    entries = jax.random.normal(rng, shape, jnp.float32) * scale * level
    return jnp.minimum(jnp.maximum(entries, -most), most).astype(held_as)


def setup_inputs(seed: int = 0) -> dict:
    key_of = jax.random.split(jax.random.key(seed), 5)
    return {
        "token_ids": with_ends(ranked(key_of[0], (TOKENS,), VALID, 2), jax.random.fold_in(key_of[0], 3), 0, VALID - 1).astype(jnp.int32),
        "head_input": noise(key_of[1], (TOKENS, D), 1.0, 6.0, ((0, 8), (1, 4))),
        "embed_grad": noise(key_of[2], (TOKENS, D), 0.3, 4.0, ((0, 8), (1, 4))),
        "logit_grad": noise(key_of[3], (TOKENS, VOCAB), TOKENS ** -0.5, 0.125, ((0, 32), (1, 8))),
    }


def reference(token_ids, head_input, embed_grad, logit_grad):
    blocks = N_TENSOR
    block_width = VOCAB // N_TENSOR
    grad_blocks = logit_grad.reshape(TOKENS, blocks, block_width).transpose(1, 0, 2)
    block_starts = jnp.arange(blocks, dtype=jnp.int32) * block_width
    embed_float = embed_grad.astype(jnp.float32)

    def one_block(block_item):
        block_grad, block_start = block_item
        head_term = lax.dot_general(block_grad, head_input, (((0,), (0,)), ((), ())), preferred_element_type=jnp.float32)
        local_ids = token_ids.astype(jnp.int32) - block_start
        inside = (local_ids >= 0) & (local_ids < block_width)
        segment = jnp.where(inside, local_ids, block_width).astype(jnp.int32)
        embed_term = jax.ops.segment_sum(embed_float, segment, num_segments=block_width + 1)[:block_width]
        row_index = block_start + jnp.arange(block_width, dtype=jnp.int32)
        summed = jnp.where((row_index < VALID)[:, None], head_term + embed_term, jnp.zeros((), jnp.float32))
        return summed.astype(jnp.bfloat16)

    tied = lax.map(one_block, (grad_blocks, block_starts))
    return tied.reshape(VOCAB, D)
```

```python
import jax
import jax.numpy as jnp
from jax import lax
from jax.experimental import pallas as pl
from jax.experimental.pallas import tpu as pltpu
from jax.sharding import Mesh, PartitionSpec as P

VALID = 50257
TILE = 128
HALF = 3200
CHUNKS = {"A": (4, 5), "B": (4, 5), "S": (7,)}
PLACES = (0, 3, 1, 2)
BIG = pltpu.CompilerParams(vmem_limit_bytes=48 << 20)
CONTRACT_ROWS = (((0,), (0,)), ((), ()))


def moved(x, axis, n, by):
    return lax.ppermute(x, axis, [(i, (i + by) % n) for i in range(n)])


def spread(x, axis):
    return [x, moved(x, axis, 4, 1), moved(x, axis, 4, -1), moved(x, axis, 4, 2)]


def turn(x, axis):
    pairs = [(i * 2 + core, (i + (3 if core else 1)) % 4 * 2 + core) for i in range(4) for core in range(2)]
    return lax.ppermute(x, (axis, "core"), pairs)


def z_pairs():
    pairs = []
    for at in range(8):
        other = (at - 1) % 8 if at % 2 == 0 else (at + 1) % 8
        for core, to in ((0, at ^ 1), (1, other)):
            pairs.append((at % 2 * 8 + at // 2 * 2 + core, to % 2 * 8 + to // 2 * 2 + core))
    return pairs


def whole(a):
    return pl.BlockSpec(a.shape, lambda i, info, n=len(a.shape): (0,) * n)


ANY = pl.BlockSpec(memory_space=pl.ANY)
SCALAR = pl.BlockSpec(memory_space=pltpu.SMEM)


def call(kernel, info, args, outs, in_specs, out_specs, grid=1, scratch=(), flops=0, **more):
    return pl.pallas_call(
        kernel,
        grid_spec=pltpu.PrefetchScalarGridSpec(
            num_scalar_prefetch=1, grid=(grid,), in_specs=in_specs, out_specs=out_specs, scratch_shapes=scratch
        ),
        out_shape=outs,
        compiler_params=BIG,
        cost_estimate=pl.CostEstimate(flops=flops, bytes_accessed=8 << 20, transcendentals=0),
        **more,
    )(info, *args)


def pack_kernel(info, head, emb, logits, ids, out, kept, given):
    rows = pl.ds(pl.multiple_of(info[3] * 128, 128), 128)
    for at, mat in enumerate((head, emb)):
        for x in range(4):
            for z in range(2):
                out[x, at * 128 : (at + 1) * 128, z * 384 : (z + 1) * 384] = mat[
                    rows, (z * 4 + x) * 384 : (z * 4 + x + 1) * 384
                ]
    cut = CHUNKS["A"][0] * TILE
    for out, z in ((kept, info[2]), (given, 1 - info[2])):
        out[:, :cut] = logits[:, pl.ds(pl.multiple_of(z * HALF, TILE), cut)]
        out[:, cut : cut + TILE] = ids[...]
        out[:, cut + TILE :] = logits[:, pl.ds(pl.multiple_of(z * HALF + cut, TILE), HALF - cut)]


def arrange(kind, info, mat, rows):
    y, x, z_lo, core = info[0], info[1], info[2], info[3]
    turned = 2 * core + 3
    for outer in range(4):
        for inner in range(4):
            if kind == "S":
                yy, xx = outer, inner
            elif kind == "A":
                yy, xx = lax.rem(y + PLACES[inner], 4), lax.rem(x + outer * turned, 4)
            else:
                yy, xx = lax.rem(y + outer * turned, 4), lax.rem(x + PLACES[inner], 4)
            for side in range(2):
                z = z_lo if side == 0 else 1 - z_lo
                source = xx % 2 * 64 if kind == "S" else pl.multiple_of(lax.rem(xx, 2) * 64, 64)
                at = outer * 512 + inner * 128 + side * 64
                rows[at : at + 64, :] = mat[yy // 2, xx // 2, yy % 2 * 2 + z, pl.ds(source, 64), :]


def join_kernel(info, mine, theirs, mine_swap, theirs_swap, i0, i1, i2, i3, head, picked, target, count, emb, rows):
    core, z_lo, first = info[3], info[2], info[4]
    for at, out in enumerate((head, emb)):
        part = slice(at * 128, (at + 1) * 128)
        out[z_lo, core] = mine[:, part]
        out[1 - z_lo, core] = theirs[:, part]
        out[z_lo, 1 - core] = mine_swap[:, part]
        out[1 - z_lo, 1 - core] = theirs_swap[:, part]
    arrange("A", info, emb, rows)
    lane = lax.broadcasted_iota(jnp.int32, (512, TILE), 1)
    below = lax.broadcasted_iota(jnp.int32, (512, 512), 0) > lax.broadcasted_iota(jnp.int32, (512, 512), 1)
    below = jnp.where(below, 1.0, 0.0).astype(jnp.bfloat16)
    total = jnp.float32(0.0)
    ranks, codes = [], []
    for piece in (i0, i1, i2, i3):
        parts = piece[...].astype(jnp.float32)
        token = jnp.sum(jnp.where(lane == 0, parts * 256.0, jnp.where(lane == 1, parts, 0.0)), axis=1, keepdims=True)
        place = token.astype(jnp.int32) - first
        inside = (place >= 0) & (place < HALF)
        mask = jnp.where(jnp.broadcast_to(inside, (512, TILE)), 1.0, 0.0)
        before = jnp.dot(below, mask.astype(jnp.bfloat16), preferred_element_type=jnp.float32)[:, :1]
        ranks.append(jnp.where(inside, (before + total).astype(jnp.int32), -1))
        total += jnp.sum(mask[:, :1])
        code = jnp.where(lane == 0, place // 64, jnp.where(lane == 1, place % 64, 0))
        codes.append(jnp.where(inside, code, 0).astype(jnp.float32).astype(jnp.bfloat16))
    blocks = (total.astype(jnp.int32) + 255) // 256
    count[0] = blocks
    for block in range(8):

        @pl.when(block < blocks)
        def _(block=block):
            slot = block * 256 + lax.broadcasted_iota(jnp.int32, (512, 256), 1)
            some, where = jnp.zeros((256, 768), jnp.float32), jnp.zeros((TILE, 256), jnp.float32)
            for p in range(4):
                pick = jnp.where(ranks[p] == slot, 1.0, 0.0).astype(jnp.bfloat16)
                some += lax.dot_general(
                    pick, rows[p * 512 : (p + 1) * 512, :], CONTRACT_ROWS, preferred_element_type=jnp.float32
                )
                where += lax.dot_general(codes[p], pick, CONTRACT_ROWS, preferred_element_type=jnp.float32)
            picked[block] = some.astype(jnp.bfloat16)
            target[block] = jnp.broadcast_to(where[0:1] * 64.0 + where[1:2], (8, 256)).astype(jnp.int32)


def grad_kernel(kind, at, parts, info, *refs):
    pieces, (head, picked, target, count) = refs[:parts], refs[parts : parts + 4]
    own, send, rows, acc = refs[-4:]
    step = pl.program_id(0)
    tile = acc.shape[0]

    @pl.when(step == 0)
    def _():
        arrange(kind, info, head, rows)

    total, row = None, 0
    for piece in pieces:
        depth = piece.shape[0]
        part = lax.dot_general(
            piece[...], rows[row : row + depth, :], CONTRACT_ROWS, preferred_element_type=jnp.float32
        )
        total = part if total is None else total + part
        row += depth
    acc[...] = total
    start = at + step * tile

    def add(block, _):
        here = start + lax.broadcasted_iota(jnp.int32, (tile, 256), 0)
        hot = jnp.where(here == target[block][:1], 1.0, 0.0).astype(jnp.bfloat16)
        acc[...] += jnp.dot(hot, picked[block], preferred_element_type=jnp.float32)
        return 0

    lax.fori_loop(0, count[0], add, 0)
    here = info[4] + start + lax.broadcasted_iota(jnp.int32, (tile, 768), 0)
    result = jnp.where(here < VALID, acc[...], 0.0).astype(jnp.bfloat16)
    low, high = result[:, :384], result[:, 384:]
    own[...] = jnp.where(info[2] == 0, low, high)
    send[...] = jnp.where(info[2] == 0, high, low)


def grad_chunk(kind, at, info, pieces, width, joined, before):
    tile = 256 if width % 256 == 0 else width
    head, picked, target, count = joined

    def kernel(*refs):
        grad_kernel(kind, at, len(pieces), *refs)

    out = jax.ShapeDtypeStruct((width, 384), jnp.bfloat16)
    return call(
        kernel,
        info,
        [*pieces, head, picked, target, count, *before],
        [out, out],
        [
            pl.BlockSpec((p.shape[0], tile), lambda i, info: (0, i))
            for p in pieces
        ]
        + [whole(head), whole(picked), whole(target), SCALAR]
        + [ANY] * len(before),
        [pl.BlockSpec((tile, 384), lambda i, info: (i, 0))] * 2,
        grid=width // tile,
        scratch=[pltpu.VMEM((2048, 768), jnp.bfloat16), pltpu.VMEM((tile, 768), jnp.float32)],
        flops=2 * 2304 * 768 * width,
    )


def local(token_ids, head_input, embed_grad, logit_grad):
    y, x = lax.axis_index("y"), lax.axis_index("x")
    z_lo, core = lax.axis_index("zl"), lax.axis_index("core")
    offset = (lax.axis_index("zh") * 2 + core) * 6400 + z_lo * HALF
    info = jnp.stack([y, x, z_lo, core, offset]).astype(jnp.int32)
    coded = jnp.stack([token_ids // 256, token_ids % 256], axis=1).astype(jnp.bfloat16)
    coded = jnp.pad(coded, ((0, 0), (0, TILE - 2)))
    half = jax.ShapeDtypeStruct((64, TILE + HALF), jnp.bfloat16)
    blocks = jax.ShapeDtypeStruct((4, 256, 768), jnp.bfloat16)
    args = [head_input, embed_grad, logit_grad, coded]
    packed, kept, given = call(
        pack_kernel, info, args, [blocks, half, half], [whole(a) for a in args], [whole(blocks), whole(half), whole(half)]
    )
    taken = moved(given, "zl", 2, 1)
    mine = lax.all_to_all(packed, "x", split_axis=0, concat_axis=0, tiled=True)
    wide = {k: sum(CHUNKS[k]) * TILE for k in "ABS"}
    a_end = TILE + wide["A"]
    b_end = a_end + wide["B"]

    def pair(start, end):
        return jnp.concatenate([kept[:, start:end], taken[:, start:end]], axis=0)

    full_a = jnp.concatenate(spread(pair(0, a_end), "y"), axis=0)
    gather_s = lax.all_gather(pair(b_end, TILE + HALF), ("y", "x"), axis=0, tiled=True)
    full_b = jnp.concatenate(spread(pair(a_end, b_end), "x"), axis=0)
    theirs = lax.ppermute(mine, ("zl", "zh", "core"), z_pairs())
    mine_swap = moved(mine, "core", 2, 1)
    theirs_swap = moved(theirs, "core", 2, 1)

    def ring(block, axis):
        out = [block]
        for _ in range(3):
            out.append(turn(out[-1], axis))
        return out

    a_cut, b_cut = TILE + CHUNKS["A"][0] * TILE, CHUNKS["B"][0] * TILE
    a1, b1 = ring(full_a[:, :a_cut], "x"), ring(full_b[:, :b_cut], "y")
    a2, b2 = ring(full_a[:, a_cut:], "x"), ring(full_b[:, b_cut:], "y")

    joins = [mine, theirs, mine_swap, theirs_swap]
    full = jax.ShapeDtypeStruct((2, 2, 4, 128, 768), jnp.bfloat16)
    picked = jax.ShapeDtypeStruct((8, 256, 768), jnp.bfloat16)
    target = jax.ShapeDtypeStruct((8, 8, 256), jnp.int32)
    joined = call(
        join_kernel,
        info,
        joins + a1,
        [full, picked, target, jax.ShapeDtypeStruct((1,), jnp.int32)],
        [whole(a) for a in joins] + [pl.BlockSpec((512, TILE), lambda i, info: (0, CHUNKS["A"][0]))] * 4,
        [whole(full), whole(picked), whole(target), SCALAR],
        scratch=[pltpu.VMEM(full.shape, jnp.bfloat16), pltpu.VMEM((2048, 768), jnp.bfloat16)],
    )

    out = jnp.zeros((6400, 384), jnp.bfloat16)
    plan = (
        ("A", 0, a1, a_cut - TILE),
        ("B", wide["A"], b1, b_cut),
        ("S", wide["A"] + wide["B"], [gather_s], wide["S"]),
        ("A", a_cut - TILE, a2, a_end - a_cut),
        ("B", wide["A"] + b_cut, b2, wide["B"] - b_cut),
    )
    done, before = [], []
    for kind, at, pieces, width in plan:
        own, send = grad_chunk(kind, at, info, pieces, width, joined, before)
        before = [own]
        done.append((at, own, moved(send, "zl", 2, 1)))
    for at, own, got in done:
        out = lax.dynamic_update_slice(out, own, (z_lo * HALF + at, 0))
    for at, own, got in done:
        out = lax.dynamic_update_slice(out, got, ((1 - z_lo) * HALF + at, 0))
    return out


def solution(mesh):
    split = Mesh(mesh.devices.reshape(4, 2, 4, 4, 2), ("y", "zl", "x", "zh", "core"))
    tokens, vocab = ("y", "zl", "x"), ("zh", "core")
    placed = (P(tokens), P(("zl", "x"), "y"), P(("zl", "x"), "y"), P(tokens, vocab))
    return jax.shard_map(local, mesh=split, in_specs=placed, out_specs=P(vocab, tokens), check_vma=False)
```

```python
import jax
import jax.numpy as jnp
from jax import lax
from jax.experimental import pallas as pl
from jax.experimental.pallas import tpu as pltpu
from jax.sharding import Mesh, PartitionSpec as P

VALID = 50257
TILE = 128
HALF = 3200
CHUNKS = {"A": (3, 5, 4), "B": (4, 5, 4)}
GOING = (0, 1, 3, 2)
PLACES = (0, 3, 1, 2)
CONTRACT_ROWS = (((0,), (0,)), ((), ()))


def moved(x, axis, n, by):
    return lax.ppermute(x, axis, [(i, (i + by) % n) for i in range(n)])


def turn(ring, axis):
    pairs = [(i * 2 + core, (i + (3 if core else 1)) % 4 * 2 + core) for i in range(4) for core in range(2)]
    ring.append(lax.ppermute(ring[-1], (axis, "core"), pairs))


def z_pairs():
    pairs = []
    for at in range(8):
        other = (at - 1) % 8 if at % 2 == 0 else (at + 1) % 8
        for core, to in ((0, at ^ 1), (1, other)):
            pairs.append((at % 2 * 8 + at // 2 * 2 + core, to % 2 * 8 + to // 2 * 2 + core))
    return pairs


def whole(a):
    return pl.BlockSpec(a.shape, lambda i, info, n=len(a.shape): (0,) * n, pipeline_mode=pl.Buffered(1))


ANY = pl.BlockSpec(memory_space=pl.ANY)
SCALAR = pl.BlockSpec(memory_space=pltpu.SMEM)


def call(kernel, info, args, outs, in_specs, out_specs, grid=1, scratch=(), flops=0, vmem=24, **more):
    return pl.pallas_call(
        kernel,
        grid_spec=pltpu.PrefetchScalarGridSpec(
            num_scalar_prefetch=1, grid=(grid,), in_specs=in_specs, out_specs=out_specs, scratch_shapes=scratch
        ),
        out_shape=outs,
        compiler_params=pltpu.CompilerParams(vmem_limit_bytes=vmem << 20),
        cost_estimate=pl.CostEstimate(flops=flops, bytes_accessed=2 << 20, transcendentals=0),
        **more,
    )(info, *args)


def edges(kind):
    sizes = [tiles * TILE for tiles in CHUNKS[kind]]
    if kind == "A":
        sizes.insert(1, TILE)
    marks = [sum(sizes[:i]) for i in range(len(sizes) + 1)]
    out = list(zip(marks[:-1], marks[1:]))
    return out if kind == "B" else [(out[0][0], out[1][1])] + out[2:]


WIDE_A = sum(CHUNKS["A"]) * TILE + TILE
WIDE_B = HALF + TILE - WIDE_A
IDS_AT = CHUNKS["A"][0] * TILE


def pack_kernel(info, head_hbm, emb_hbm, logits_hbm, ids, *refs):
    outs, (head, emb, logits, sems) = refs[:6], refs[6:]
    mine = pl.ds(pl.multiple_of(info[3] * 128, 128), 128)
    loads = [
        pltpu.make_async_copy(logits_hbm, logits, sems.at[0]),
        pltpu.make_async_copy(head_hbm.at[mine, :], head, sems.at[1]),
        pltpu.make_async_copy(emb_hbm.at[mine, :], emb, sems.at[2]),
    ]
    for load in loads:
        load.start()
    loads[0].wait()
    kept, given = outs[4:]
    cut = IDS_AT
    for half, z in ((kept, info[2]), (given, 1 - info[2])):
        half[:, :cut] = logits[:, pl.ds(pl.multiple_of(z * HALF, TILE), cut)]
        half[:, cut : cut + TILE] = ids[...]
        half[:, cut + TILE :] = logits[:, pl.ds(pl.multiple_of(z * HALF + cut, TILE), HALF - cut)]
    loads[1].wait()
    loads[2].wait()
    for out, away in zip(outs[:4], GOING):
        x = lax.rem(info[1] + away, 4)
        for at, mat in enumerate((head, emb)):
            for z in range(2):
                start = pl.multiple_of((z * 4 + x) * 384, 128)
                out[at * 128 : (at + 1) * 128, z * 384 : (z + 1) * 384] = mat[:, pl.ds(start, 384)]


def pair_kernel(start, end, info, kept, taken, *rest):
    out = rest[-1]
    for half, z in ((kept, info[2]), (taken, 1 - info[2])):
        out[pl.ds(pl.multiple_of(z * 64, 64), 64), :] = half[:, start:end]


def stack_kernel(spans, parts, info, *refs):
    for i, (start, end) in enumerate(spans):
        for p in range(4):
            refs[parts + i][p * 128 : (p + 1) * 128, :] = refs[i * 4 + p][:, start:end]


def block_of(mat, y, x, z):
    at = x % 2 * 64
    at = at if isinstance(at, int) else pl.multiple_of(at, 64)
    return mat[y // 2, x // 2, y % 2 * 2 + z, pl.ds(at, 64), :]


def place_of(kind, info, outer, inner):
    turned = 2 * info[3] + 3
    y, x = (inner, outer) if kind == "A" else (outer, inner)
    return lax.rem(info[0] + y * turned, 4), lax.rem(info[1] + x * turned, 4)


def by_x_kernel(info, *refs):
    out = refs[-1]
    for block, place in zip(refs[:4], PLACES):
        out[lax.rem(info[1] + place, 4)] = block[...]


def relay_kernel(info, *refs):
    refs[-1][...] = refs[0][...]


def join(info, refs, out, part):
    core, z_lo = info[3], info[2]
    mine, theirs, mine_swap, theirs_swap = refs
    rows = slice(part * 128, (part + 1) * 128)
    out[z_lo, core] = mine[:, rows]
    out[1 - z_lo, core] = theirs[:, rows]
    out[z_lo, 1 - core] = mine_swap[:, rows]
    out[1 - z_lo, 1 - core] = theirs_swap[:, rows]


def head_kernel(info, *refs):
    head_t, emb, head = refs[4:]
    join(info, refs[:4], head, 0)
    join(info, refs[:4], emb, 1)
    for y in range(4):
        for x in range(4):
            both = jnp.concatenate([block_of(head, y, x, 0), block_of(head, y, x, 1)], axis=0)
            head_t[y, x] = both.T


def embed_kernel(info, *refs):
    pieces = refs[:4]
    emb, picked, target, more_picked, more_target, count, rows, ids, sem, sems = refs[4:]
    first = info[4]
    loads = [
        pltpu.make_async_copy(piece.at[:, pl.ds(IDS_AT, TILE)], ids.at[p], sems.at[p]) for p, piece in enumerate(pieces)
    ]
    for load in loads:
        load.start()
    for outer in range(4):
        for inner in range(4):
            y, x = place_of("A", info, outer, inner)
            for z in range(2):
                at = outer * 512 + inner * 128 + z * 64
                rows[at : at + 64, :768] = block_of(emb, y, x, z)
    for load in loads:
        load.wait()
    lane = lax.broadcasted_iota(jnp.int32, (512, TILE), 1)
    below = lax.broadcasted_iota(jnp.int32, (512, 512), 0) > lax.broadcasted_iota(jnp.int32, (512, 512), 1)
    below = jnp.where(below, 1.0, 0.0).astype(jnp.bfloat16)
    total = jnp.float32(0.0)
    ranks = []
    for p in range(4):
        parts = ids[p].astype(jnp.float32)
        token = jnp.sum(jnp.where(lane == 0, parts * 256.0, jnp.where(lane == 1, parts, 0.0)), axis=1, keepdims=True)
        place = token.astype(jnp.int32) - first
        inside = (place >= 0) & (place < HALF)
        mask = jnp.where(jnp.broadcast_to(inside, (512, TILE)), 1.0, 0.0)
        before = jnp.dot(below, mask.astype(jnp.bfloat16), preferred_element_type=jnp.float32)[:, :1]
        ranks.append(jnp.where(inside, (before + total).astype(jnp.int32), -1))
        total += jnp.sum(mask[:, :1])
        code = jnp.where(lane == 0, place // 64, jnp.where(lane == 1, place % 64, 0))
        code = jnp.where(inside, code, 0).astype(jnp.float32).astype(jnp.bfloat16)
        rows[p * 512 : (p + 1) * 512, 768:] = code
    blocks = (total.astype(jnp.int32) + 255) // 256
    count[0] = blocks

    def fill(block):
        slot = block * 256 + lax.broadcasted_iota(jnp.int32, (512, 256), 1)
        some = jnp.zeros((256, 768 + TILE), jnp.float32)
        for p in range(4):
            pick = jnp.where(ranks[p] == slot, 1.0, 0.0).astype(jnp.bfloat16)
            some += lax.dot_general(
                pick, rows[p * 512 : (p + 1) * 512, :], CONTRACT_ROWS, preferred_element_type=jnp.float32
            )
        picked[...] = some[:, :768].astype(jnp.bfloat16).T
        where = some[:, 768:769] * 64.0 + some[:, 769:770]
        target[...] = jnp.broadcast_to(where, (256, TILE)).astype(jnp.int32)

    for block in range(7, 0, -1):

        @pl.when(block < blocks)
        def _(block=block):
            fill(block)
            one = pltpu.make_async_copy(picked, more_picked.at[block - 1], sem)
            one.start()
            one.wait()
            two = pltpu.make_async_copy(target, more_target.at[block - 1], sem)
            two.start()
            two.wait()

    fill(0)


def grad_kernel(kind, at, chained, info, *refs):
    pieces, (head_t, picked, target, more_picked, more_target, count) = refs[:4], refs[4:10]
    out, send, acc, ready, next_picked, next_target, sem = refs[10 + chained :]
    width = acc.shape[1]
    total = None
    for outer, piece in enumerate(pieces):
        left = []
        for inner in range(4):
            y, x = place_of(kind, info, outer, inner)
            left.append(head_t[y, x])
        part = jnp.dot(jnp.concatenate(left, axis=1), piece[:, :width], preferred_element_type=jnp.float32)
        total = part if total is None else total + part

    def term(some, where):
        here = at + lax.broadcasted_iota(jnp.int32, (256, width), 1)
        hot = jnp.where(here == where[:, :1], 1.0, 0.0).astype(jnp.bfloat16)
        return jnp.dot(some, hot, preferred_element_type=jnp.float32)

    acc[...] = total + term(picked[...], target[...])

    def add(block, _):
        one = pltpu.make_async_copy(more_picked.at[block], next_picked, sem)
        one.start()
        one.wait()
        two = pltpu.make_async_copy(more_target.at[block], next_target, sem)
        two.start()
        two.wait()
        acc[...] += term(next_picked[...], next_target[...])
        return 0

    lax.fori_loop(0, count[0] - 1, add, 0)
    here = info[4] + at + lax.broadcasted_iota(jnp.int32, (768, width), 1)
    result = jnp.where(here < VALID, acc[...], 0.0).astype(jnp.bfloat16)
    low, high = result[:384], result[384:]
    ready[...] = jnp.where(info[2] == 0, low, high).T
    here = pl.multiple_of(info[2] * HALF + at, TILE)
    copy = pltpu.make_async_copy(ready, out.at[pl.ds(here, width), :], sem)
    copy.start()
    send[...] = jnp.where(info[2] == 0, high, low).T
    copy.wait()


def grad_chunk(kind, at, info, pieces, width, joined, out):
    head_t, picked, target, more_picked, more_target, count = joined
    chained = 0 if out is None else 1

    def kernel(*refs):
        grad_kernel(kind, at, chained, *refs)

    sent = shaped(width, 384)
    return call(
        kernel,
        info,
        [*pieces, head_t, picked, target, more_picked, more_target, count] + [out] * chained,
        [shaped(2 * HALF, 384), sent],
        [whole(p) for p in pieces] + [whole(head_t), whole(picked), whole(target), ANY, ANY, SCALAR] + [ANY] * chained,
        [ANY, whole(sent)],
        scratch=[
            pltpu.VMEM((768, width), jnp.float32),
            pltpu.VMEM((width, 384), jnp.bfloat16),
            pltpu.VMEM((768, 256), jnp.bfloat16),
            pltpu.VMEM((256, TILE), jnp.int32),
            pltpu.SemaphoreType.DMA,
        ],
        flops=2 * 2304 * 768 * width,
        input_output_aliases={11: 0} if chained else {},
    )


def shaped(*dims):
    return jax.ShapeDtypeStruct(dims, jnp.bfloat16)


def stack(info, groups, spans, before=()):
    args = [a for group in groups for a in group]
    outs = [shaped(512, end - start) for start, end in spans]
    parts = len(args) + len(before)
    return call(
        lambda *refs: stack_kernel(spans, parts, *refs),
        info,
        [*args, *before],
        outs,
        [whole(a) for a in args] + [ANY] * len(before),
        [whole(a) for a in outs],
    )


def local(token_ids, head_input, embed_grad, logit_grad):
    y, x = lax.axis_index("y"), lax.axis_index("x")
    z_lo, core = lax.axis_index("zl"), lax.axis_index("core")
    offset = (lax.axis_index("zh") * 2 + core) * 6400 + z_lo * HALF
    info = jnp.stack([y, x, z_lo, core, offset]).astype(jnp.int32)
    coded = jnp.stack([token_ids // 256, token_ids % 256], axis=1).astype(jnp.bfloat16)
    coded = jnp.pad(coded, ((0, 0), (0, TILE - 2)))
    half, block = shaped(64, TILE + HALF), shaped(256, 768)
    args = [head_input, embed_grad, logit_grad, coded]
    outs = [block] * 4 + [half, half]
    *blocks, kept, given = call(
        pack_kernel,
        info,
        args,
        outs,
        [ANY, ANY, ANY, whole(coded)],
        [whole(a) for a in outs],
        scratch=[
            pltpu.VMEM((128, 3072), jnp.bfloat16),
            pltpu.VMEM((128, 3072), jnp.bfloat16),
            pltpu.VMEM((64, 6400), jnp.bfloat16),
            pltpu.SemaphoreType.DMA((3,)),
        ],
    )
    taken = moved(given, "zl", 2, 1)
    blocks = [blocks[0]] + [moved(b, "x", 4, by) for b, by in zip(blocks[1:], GOING[1:])]

    def pair(start, end, before=()):
        out = shaped(128, end - start)
        return call(
            lambda *refs: pair_kernel(start, end, *refs),
            info,
            [kept, taken, *before],
            [out],
            [whole(half)] * 2 + [ANY] * len(before),
            [whole(out)],
        )[0]

    def relay(a, before):
        specs = [whole(a)] + [ANY] * len(before)
        return call(relay_kernel, info, [a, *before], [shaped(*a.shape)], specs, [whole(a)])[0]

    all_a, all_b = [pair(0, WIDE_A)], [pair(WIDE_A, WIDE_A + WIDE_B)]
    for _ in range(3):
        turn(all_a, "y")
        turn(all_b, "x")
    out = shaped(4, 256, 768)
    mine = call(by_x_kernel, info, [*blocks, all_a[0]], [out], [whole(block)] * 4 + [ANY], [whole(out)])[0]
    theirs = lax.ppermute(mine, ("zl", "zh", "core"), z_pairs())
    mine_swap = moved(mine, "core", 2, 1)
    theirs_swap = moved(theirs, "core", 2, 1)
    joins = [mine, theirs, mine_swap, theirs_swap]

    parts = shaped(2, 2, 4, 128, 768)
    outs = [shaped(4, 4, 768, 128), parts]
    head_t, emb = call(
        head_kernel,
        info,
        joins,
        outs,
        [whole(a) for a in joins],
        [whole(a) for a in outs],
        scratch=[pltpu.VMEM(parts.shape, jnp.bfloat16)],
    )

    spans_a, spans_b = edges("A"), edges("B")
    a1 = list(stack(info, [all_a], spans_a[:1]))
    b1 = list(stack(info, [all_b], spans_b[:1]))
    for _ in range(2):
        turn(a1, "x")
        turn(b1, "y")
    a2 = list(stack(info, [all_a], spans_a[1:2], [a1[2], head_t]))
    b2 = list(stack(info, [all_b], spans_b[1:2], [b1[2], head_t]))
    for ring, axis in ((a1, "x"), (b1, "y"), (a2, "x"), (b2, "y"), (a2, "x"), (b2, "y")):
        turn(ring, axis)
    one = [shaped(768, 256), jax.ShapeDtypeStruct((256, TILE), jnp.int32)]
    more = [shaped(7, 768, 256), jax.ShapeDtypeStruct((7, 256, TILE), jnp.int32)]
    joined = call(
        embed_kernel,
        info,
        [*a1, emb],
        one + more + [jax.ShapeDtypeStruct((1,), jnp.int32)],
        [ANY] * 4 + [whole(emb)],
        [whole(a) for a in one] + [ANY, ANY, SCALAR],
        scratch=[
            pltpu.VMEM((2048, 768 + TILE), jnp.bfloat16),
            pltpu.VMEM((4, 512, TILE), jnp.bfloat16),
            pltpu.SemaphoreType.DMA,
            pltpu.SemaphoreType.DMA((4,)),
        ],
    )
    joined = [head_t, *joined]
    got = []

    def finish(kind, i, pieces, out):
        sizes = [tiles * TILE for tiles in CHUNKS[kind]]
        at = sum(sizes[:i]) + (0 if kind == "A" else WIDE_A - TILE)
        out, send = grad_chunk(kind, at, info, pieces, sizes[i], joined, out)
        got.append((at, moved(send, "zl", 2, 1)))
        return out, send

    out, send_a = finish("A", 0, a1, None)
    out, send_b = finish("B", 0, b1, out)
    a3 = list(stack(info, [all_a], spans_a[2:], [a2[2]]))
    b3 = list(stack(info, [all_b], spans_b[2:], [b2[2]]))
    for ring, axis in ((a2, "x"), (b2, "y"), (a3, "x"), (b3, "y")):
        turn(ring, axis)
    a3[1] = relay(a3[1], [send_a])
    b3[1] = relay(b3[1], [send_b])
    for ring, axis in ((a3, "x"), (b3, "y"), (a3, "x"), (b3, "y")):
        turn(ring, axis)
    out, _ = finish("A", 1, a2, out)
    out, _ = finish("B", 1, b2, out)
    out, _ = finish("A", 2, a3, out)
    out, _ = finish("B", 2, b3, out)
    for at, part in got:
        out = lax.dynamic_update_slice(out, part, ((1 - z_lo) * HALF + at, 0))
    return out


def solution(mesh):
    split = Mesh(mesh.devices.reshape(4, 2, 4, 4, 2), ("y", "zl", "x", "zh", "core"))
    tokens, vocab = ("y", "zl", "x"), ("zh", "core")
    placed = (P(tokens), P(("zl", "x"), "y"), P(("zl", "x"), "y"), P(tokens, vocab))
    return jax.shard_map(local, mesh=split, in_specs=placed, out_specs=P(vocab, tokens), check_vma=False)
```

```python
import jax
import jax.numpy as jnp
from jax import lax
from jax.experimental import pallas as pl
from jax.experimental.pallas import tpu as pltpu
from jax.sharding import Mesh, PartitionSpec as P

VALID = 50257
TILE = 128
HALF = 3200
CHUNKS = {"A": (4, 8), "B": (5, 8)}
GOING = (0, 1, 3, 2)
PLACES = (0, 3, 1, 2)
CONTRACT_ROWS = (((0,), (0,)), ((), ()))


def moved(x, axis, n, by):
    return lax.ppermute(x, axis, [(i, (i + by) % n) for i in range(n)])


def turn(ring, axis):
    pairs = [(i * 2 + core, (i + (3 if core else 1)) % 4 * 2 + core) for i in range(4) for core in range(2)]
    ring.append(lax.ppermute(ring[-1], (axis, "core"), pairs))


def z_pairs():
    pairs = []
    for at in range(8):
        other = (at - 1) % 8 if at % 2 == 0 else (at + 1) % 8
        for core, to in ((0, at ^ 1), (1, other)):
            pairs.append((at % 2 * 8 + at // 2 * 2 + core, to % 2 * 8 + to // 2 * 2 + core))
    return pairs


def whole(a):
    return pl.BlockSpec(a.shape, lambda i, info, n=len(a.shape): (0,) * n, pipeline_mode=pl.Buffered(1))


ANY = pl.BlockSpec(memory_space=pl.ANY)
SCALAR = pl.BlockSpec(memory_space=pltpu.SMEM)


def call(kernel, info, args, outs, in_specs, out_specs, grid=1, scratch=(), flops=0, vmem=24, **more):
    return pl.pallas_call(
        kernel,
        grid_spec=pltpu.PrefetchScalarGridSpec(
            num_scalar_prefetch=1, grid=(grid,), in_specs=in_specs, out_specs=out_specs, scratch_shapes=scratch
        ),
        out_shape=outs,
        compiler_params=pltpu.CompilerParams(vmem_limit_bytes=vmem << 20),
        cost_estimate=pl.CostEstimate(flops=flops, bytes_accessed=2 << 20, transcendentals=0),
        **more,
    )(info, *args)


def edges(kind):
    sizes = [tiles * TILE for tiles in CHUNKS[kind]]
    if kind == "A":
        sizes.insert(1, TILE)
    marks = [sum(sizes[:i]) for i in range(len(sizes) + 1)]
    out = list(zip(marks[:-1], marks[1:]))
    return out if kind == "B" else [(out[0][0], out[1][1])] + out[2:]


WIDE_A = sum(CHUNKS["A"]) * TILE + TILE
WIDE_B = HALF + TILE - WIDE_A
IDS_AT = CHUNKS["A"][0] * TILE


def pack_kernel(info, head_hbm, emb_hbm, logits_hbm, ids, *refs):
    outs, (head, emb, logits, sems) = refs[:6], refs[6:]
    mine = pl.ds(pl.multiple_of(info[3] * 128, 128), 128)
    loads = [
        pltpu.make_async_copy(logits_hbm, logits, sems.at[0]),
        pltpu.make_async_copy(head_hbm.at[mine, :], head, sems.at[1]),
        pltpu.make_async_copy(emb_hbm.at[mine, :], emb, sems.at[2]),
    ]
    for load in loads:
        load.start()
    loads[0].wait()
    kept, given = outs[4:]
    cut = IDS_AT
    for half, z in ((kept, info[2]), (given, 1 - info[2])):
        half[:, :cut] = logits[:, pl.ds(pl.multiple_of(z * HALF, TILE), cut)]
        half[:, cut : cut + TILE] = ids[...]
        half[:, cut + TILE :] = logits[:, pl.ds(pl.multiple_of(z * HALF + cut, TILE), HALF - cut)]
    loads[1].wait()
    loads[2].wait()
    for out, away in zip(outs[:4], GOING):
        x = lax.rem(info[1] + away, 4)
        for at, mat in enumerate((head, emb)):
            for z in range(2):
                start = pl.multiple_of((z * 4 + x) * 384, 128)
                out[at * 128 : (at + 1) * 128, z * 384 : (z + 1) * 384] = mat[:, pl.ds(start, 384)]


def pair_kernel(start, end, info, kept, taken, *rest):
    out = rest[-1]
    for half, z in ((kept, info[2]), (taken, 1 - info[2])):
        out[pl.ds(pl.multiple_of(z * 64, 64), 64), :] = half[:, start:end]


def stack_kernel(spans, parts, info, *refs):
    for i, (start, end) in enumerate(spans):
        for p in range(4):
            refs[parts + i][p * 128 : (p + 1) * 128, :] = refs[i * 4 + p][:, start:end]


def block_of(mat, y, x, z):
    at = x % 2 * 64
    at = at if isinstance(at, int) else pl.multiple_of(at, 64)
    return mat[y // 2, x // 2, y % 2 * 2 + z, pl.ds(at, 64), :]


def place_of(kind, info, outer, inner):
    turned = 2 * info[3] + 3
    y, x = (inner, outer) if kind == "A" else (outer, inner)
    return lax.rem(info[0] + y * turned, 4), lax.rem(info[1] + x * turned, 4)


def by_x_kernel(info, *refs):
    out = refs[-1]
    for block, place in zip(refs[:4], PLACES):
        out[lax.rem(info[1] + place, 4)] = block[...]


def relay_kernel(info, *refs):
    refs[-1][...] = refs[0][...]


def join(info, refs, out, part):
    core, z_lo = info[3], info[2]
    mine, theirs, mine_swap, theirs_swap = refs
    rows = slice(part * 128, (part + 1) * 128)
    out[z_lo, core] = mine[:, rows]
    out[1 - z_lo, core] = theirs[:, rows]
    out[z_lo, 1 - core] = mine_swap[:, rows]
    out[1 - z_lo, 1 - core] = theirs_swap[:, rows]


def head_kernel(info, *refs):
    head_t, emb, head = refs[4:]
    join(info, refs[:4], head, 0)
    join(info, refs[:4], emb, 1)
    for y in range(4):
        for x in range(4):
            both = jnp.concatenate([block_of(head, y, x, 0), block_of(head, y, x, 1)], axis=0)
            head_t[y, x] = both.T


def embed_kernel(info, *refs):
    pieces = refs[:4]
    emb, picked, target, more_picked, more_target, count, rows, ids, sem, sems = refs[4:]
    first = info[4]
    loads = [
        pltpu.make_async_copy(piece.at[:, pl.ds(IDS_AT, TILE)], ids.at[p], sems.at[p]) for p, piece in enumerate(pieces)
    ]
    for load in loads:
        load.start()
    for outer in range(4):
        for inner in range(4):
            y, x = place_of("A", info, outer, inner)
            for z in range(2):
                at = outer * 512 + inner * 128 + z * 64
                rows[at : at + 64, :768] = block_of(emb, y, x, z)
    for load in loads:
        load.wait()
    lane = lax.broadcasted_iota(jnp.int32, (512, TILE), 1)
    below = lax.broadcasted_iota(jnp.int32, (512, 512), 0) > lax.broadcasted_iota(jnp.int32, (512, 512), 1)
    below = jnp.where(below, 1.0, 0.0).astype(jnp.bfloat16)
    total = jnp.float32(0.0)
    ranks = []
    for p in range(4):
        parts = ids[p].astype(jnp.float32)
        token = jnp.sum(jnp.where(lane == 0, parts * 256.0, jnp.where(lane == 1, parts, 0.0)), axis=1, keepdims=True)
        place = token.astype(jnp.int32) - first
        inside = (place >= 0) & (place < HALF)
        mask = jnp.where(jnp.broadcast_to(inside, (512, TILE)), 1.0, 0.0)
        before = jnp.dot(below, mask.astype(jnp.bfloat16), preferred_element_type=jnp.float32)[:, :1]
        ranks.append(jnp.where(inside, (before + total).astype(jnp.int32), -1))
        total += jnp.sum(mask[:, :1])
        code = jnp.where(lane == 0, place // 64, jnp.where(lane == 1, place % 64, 0))
        code = jnp.where(inside, code, 0).astype(jnp.float32).astype(jnp.bfloat16)
        rows[p * 512 : (p + 1) * 512, 768:] = code
    blocks = (total.astype(jnp.int32) + 255) // 256
    count[0] = blocks

    def fill(block):
        slot = block * 256 + lax.broadcasted_iota(jnp.int32, (512, 256), 1)
        some = jnp.zeros((256, 768 + TILE), jnp.float32)
        for p in range(4):
            pick = jnp.where(ranks[p] == slot, 1.0, 0.0).astype(jnp.bfloat16)
            some += lax.dot_general(
                pick, rows[p * 512 : (p + 1) * 512, :], CONTRACT_ROWS, preferred_element_type=jnp.float32
            )
        picked[...] = some[:, :768].astype(jnp.bfloat16).T
        where = some[:, 768:769] * 64.0 + some[:, 769:770]
        target[...] = jnp.broadcast_to(where, (256, TILE)).astype(jnp.int32)

    for block in range(7, 0, -1):

        @pl.when(block < blocks)
        def _(block=block):
            fill(block)
            one = pltpu.make_async_copy(picked, more_picked.at[block - 1], sem)
            one.start()
            one.wait()
            two = pltpu.make_async_copy(target, more_target.at[block - 1], sem)
            two.start()
            two.wait()

    fill(0)


def grad_kernel(kind, at, chained, info, *refs):
    pieces, (head_t, picked, target, more_picked, more_target, count) = refs[:4], refs[4:10]
    out, send, acc, ready, next_picked, next_target, sem = refs[10 + chained :]
    width = acc.shape[1]
    total = None
    for outer, piece in enumerate(pieces):
        left = []
        for inner in range(4):
            y, x = place_of(kind, info, outer, inner)
            left.append(head_t[y, x])
        part = jnp.dot(jnp.concatenate(left, axis=1), piece[:, :width], preferred_element_type=jnp.float32)
        total = part if total is None else total + part

    def term(some, where):
        here = at + lax.broadcasted_iota(jnp.int32, (256, width), 1)
        hot = jnp.where(here == where[:, :1], 1.0, 0.0).astype(jnp.bfloat16)
        return jnp.dot(some, hot, preferred_element_type=jnp.float32)

    acc[...] = total + term(picked[...], target[...])

    def add(block, _):
        one = pltpu.make_async_copy(more_picked.at[block], next_picked, sem)
        one.start()
        one.wait()
        two = pltpu.make_async_copy(more_target.at[block], next_target, sem)
        two.start()
        two.wait()
        acc[...] += term(next_picked[...], next_target[...])
        return 0

    lax.fori_loop(0, count[0] - 1, add, 0)
    here = info[4] + at + lax.broadcasted_iota(jnp.int32, (768, width), 1)
    result = jnp.where(here < VALID, acc[...], 0.0).astype(jnp.bfloat16)
    low, high = result[:384], result[384:]
    ready[...] = jnp.where(info[2] == 0, low, high).T
    here = pl.multiple_of(info[2] * HALF + at, TILE)
    copy = pltpu.make_async_copy(ready, out.at[pl.ds(here, width), :], sem)
    copy.start()
    send[...] = jnp.where(info[2] == 0, high, low).T
    copy.wait()


def grad_chunk(kind, at, info, pieces, block, width, joined, out):
    head_t, picked, target, more_picked, more_target, count = joined
    chained = 0 if out is None else 1

    def kernel(*refs):
        grad_kernel(kind, at, chained, *refs)

    sent = shaped(width, 384)
    return call(
        kernel,
        info,
        [*pieces, head_t, picked, target, more_picked, more_target, count] + [out] * chained,
        [shaped(2 * HALF, 384), sent],
        [
            pl.BlockSpec((p.shape[0], width), lambda i, info: (0, block), pipeline_mode=pl.Buffered(1)) for p in pieces
        ]
        + [whole(head_t), whole(picked), whole(target), ANY, ANY, SCALAR] + [ANY] * chained,
        [ANY, whole(sent)],
        scratch=[
            pltpu.VMEM((768, width), jnp.float32),
            pltpu.VMEM((width, 384), jnp.bfloat16),
            pltpu.VMEM((768, 256), jnp.bfloat16),
            pltpu.VMEM((256, TILE), jnp.int32),
            pltpu.SemaphoreType.DMA,
        ],
        flops=2 * 2304 * 768 * width,
        input_output_aliases={11: 0} if chained else {},
    )


def shaped(*dims):
    return jax.ShapeDtypeStruct(dims, jnp.bfloat16)


def stack(info, groups, spans, before=()):
    args = [a for group in groups for a in group]
    outs = [shaped(512, end - start) for start, end in spans]
    parts = len(args) + len(before)
    return call(
        lambda *refs: stack_kernel(spans, parts, *refs),
        info,
        [*args, *before],
        outs,
        [whole(a) for a in args] + [ANY] * len(before),
        [whole(a) for a in outs],
    )


def local(token_ids, head_input, embed_grad, logit_grad):
    y, x = lax.axis_index("y"), lax.axis_index("x")
    z_lo, core = lax.axis_index("zl"), lax.axis_index("core")
    offset = (lax.axis_index("zh") * 2 + core) * 6400 + z_lo * HALF
    info = jnp.stack([y, x, z_lo, core, offset]).astype(jnp.int32)
    coded = jnp.stack([token_ids // 256, token_ids % 256], axis=1).astype(jnp.bfloat16)
    coded = jnp.pad(coded, ((0, 0), (0, TILE - 2)))
    half, block = shaped(64, TILE + HALF), shaped(256, 768)
    args = [head_input, embed_grad, logit_grad, coded]
    outs = [block] * 4 + [half, half]
    *blocks, kept, given = call(
        pack_kernel,
        info,
        args,
        outs,
        [ANY, ANY, ANY, whole(coded)],
        [whole(a) for a in outs],
        scratch=[
            pltpu.VMEM((128, 3072), jnp.bfloat16),
            pltpu.VMEM((128, 3072), jnp.bfloat16),
            pltpu.VMEM((64, 6400), jnp.bfloat16),
            pltpu.SemaphoreType.DMA((3,)),
        ],
    )
    taken = moved(given, "zl", 2, 1)
    blocks = [blocks[0]] + [moved(b, "x", 4, by) for b, by in zip(blocks[1:], GOING[1:])]

    def pair(start, end, before=()):
        out = shaped(128, end - start)
        return call(
            lambda *refs: pair_kernel(start, end, *refs),
            info,
            [kept, taken, *before],
            [out],
            [whole(half)] * 2 + [ANY] * len(before),
            [whole(out)],
        )[0]

    def relay(a, before):
        specs = [whole(a)] + [ANY] * len(before)
        return call(relay_kernel, info, [a, *before], [shaped(*a.shape)], specs, [whole(a)])[0]

    all_a, all_b = [pair(0, WIDE_A)], [pair(WIDE_A, WIDE_A + WIDE_B)]
    for _ in range(3):
        turn(all_a, "y")
        turn(all_b, "x")
    out = shaped(4, 256, 768)
    mine = call(by_x_kernel, info, [*blocks, all_a[0]], [out], [whole(block)] * 4 + [ANY], [whole(out)])[0]
    theirs = lax.ppermute(mine, ("zl", "zh", "core"), z_pairs())
    mine_swap = moved(mine, "core", 2, 1)
    theirs_swap = moved(theirs, "core", 2, 1)
    joins = [mine, theirs, mine_swap, theirs_swap]

    parts = shaped(2, 2, 4, 128, 768)
    outs = [shaped(4, 4, 768, 128), parts]
    head_t, emb = call(
        head_kernel,
        info,
        joins,
        outs,
        [whole(a) for a in joins],
        [whole(a) for a in outs],
        scratch=[pltpu.VMEM(parts.shape, jnp.bfloat16)],
    )

    spans_a, spans_b = edges("A"), edges("B")
    a1 = list(stack(info, [all_a], spans_a[:1]))
    b1 = list(stack(info, [all_b], spans_b[:1]))
    for _ in range(2):
        turn(a1, "x")
        turn(b1, "y")
    a2 = list(stack(info, [all_a], spans_a[1:2], [a1[2], head_t]))
    b2 = list(stack(info, [all_b], spans_b[1:2], [b1[2], head_t]))
    for ring, axis in ((a1, "x"), (b1, "y"), (a2, "x"), (b2, "y")):
        turn(ring, axis)
    a2[1], b2[1] = relay(a2[1], [a1[3]]), relay(b2[1], [b1[3]])
    turn(a2, "x")
    turn(b2, "y")
    one = [shaped(768, 256), jax.ShapeDtypeStruct((256, TILE), jnp.int32)]
    more = [shaped(7, 768, 256), jax.ShapeDtypeStruct((7, 256, TILE), jnp.int32)]
    joined = call(
        embed_kernel,
        info,
        [*a1, emb],
        one + more + [jax.ShapeDtypeStruct((1,), jnp.int32)],
        [ANY] * 4 + [whole(emb)],
        [whole(a) for a in one] + [ANY, ANY, SCALAR],
        scratch=[
            pltpu.VMEM((2048, 768 + TILE), jnp.bfloat16),
            pltpu.VMEM((4, 512, TILE), jnp.bfloat16),
            pltpu.SemaphoreType.DMA,
            pltpu.SemaphoreType.DMA((4,)),
        ],
    )
    joined = [head_t, *joined]
    got = []

    def finish(kind, i, pieces, out, block=0, blocks=1):
        sizes = [tiles * TILE for tiles in CHUNKS[kind]]
        width = sizes[i] // blocks
        at = sum(sizes[:i]) + (0 if kind == "A" else WIDE_A - TILE) + block * width
        out, send = grad_chunk(kind, at, info, pieces, block, width, joined, out)
        got.append((at, moved(send, "zl", 2, 1)))
        return out, send

    out, send_a = finish("A", 0, a1, None)
    out, send_b = finish("B", 0, b1, out)
    a2[2], b2[2] = relay(a2[2], [send_a]), relay(b2[2], [send_b])
    turn(a2, "x")
    turn(b2, "y")
    for block in range(2):
        out, _ = finish("A", 1, a2, out, block, 2)
        out, _ = finish("B", 1, b2, out, block, 2)
    for at, part in got:
        out = lax.dynamic_update_slice(out, part, ((1 - z_lo) * HALF + at, 0))
    return out


def solution(mesh):
    split = Mesh(mesh.devices.reshape(4, 2, 4, 4, 2), ("y", "zl", "x", "zh", "core"))
    tokens, vocab = ("y", "zl", "x"), ("zh", "core")
    placed = (P(tokens), P(("zl", "x"), "y"), P(("zl", "x"), "y"), P(tokens, vocab))
    return jax.shard_map(local, mesh=split, in_specs=placed, out_specs=P(vocab, tokens), check_vma=False)
```
